32 devices in a mesh: seg: 4 (over y, core), op: 8 (over z, x).
Axes of the slice: x: 2, y: 2, z: 4, core: 2. Of those that a mesh axis runs over, the one named last changes fastest.
Arguments:
- psi_start: bfloat16 [4, 32, 128, 128], P('seg', 'op'), may hold values from -4 to 4
- left_ops: bfloat16 [4, 32, 32, 128, 128], P('seg', 'op'), may hold values from -2 to 9, as said below
- right_ops: bfloat16 [4, 32, 32, 128, 128], P('seg', 'op'), may hold values from -2 to 9, as said below
- shifts: int32 [4, 32], P('seg', 'op'), may hold values from 0 to 31
- active: int32 [4, 32, 32], P('seg', 'op'), may hold values 0 or 1
Outputs:
- state: bfloat16 [4, 32, 128, 128], P('seg', 'op')
- rdm_pieces: float32 [4, 32], P('seg', 'op')
The draws below stay inside these ranges and needn't reach their ends.
Inputs may be any that keep to these rules, and one draw needn't show every extreme that they name: `left_ops`: each block is a diagonal of entries between 1 and 7.8 plus off-diagonal entries of size about 2 / sqrt(128). `right_ops`: each block is a diagonal of entries between 1 and 7.8 plus off-diagonal entries of size about 2 / sqrt(128).
All inputs are finite; a program needn't handle non-finite values. No bound on the sum of `active` on one device may be relied on, other than what follows from the above.
Results may differ from the reference program's by a relative error of at most 0.0046.
Values may be sent and summed in bfloat16 or wider, within the bound.
No kernel may reach another device: no remote copies, remote signals or barrier semaphores. Data moves between devices by JAX's collectives and lax.ppermute only.
A program may use at most 64 MiB of HBM per device.

```python
import jax
import jax.numpy as jnp
from jax import lax

QB = 128
SECT = 32
ITERS = 3
TERMS = 32
SEGS = 4
N_SEG = 4


def dominant_blocks(key, shape, diag_low, diag_high, noise_scale, flat_noise):
    key_diag, key_noise = jax.random.split(key)
    width = shape[-1]
    diagonal = jax.random.uniform(key_diag, shape[:-1], jnp.float32, diag_low, diag_high)
    if flat_noise:
        noise = jax.random.uniform(key_noise, shape, jnp.float32, -1.7, 1.7)
    else:
        noise = jnp.clip(jax.random.normal(key_noise, shape, jnp.float32), -4.0, 4.0)
    rows = lax.broadcasted_iota(jnp.int32, (width, width), 0)
    cols = lax.broadcasted_iota(jnp.int32, (width, width), 1)
    identity = (rows == cols).astype(jnp.float32)
    return noise * (noise_scale / jnp.sqrt(float(width))) + identity * diagonal[..., None]


def draw_psi_start(key, part):
    shape = (SEGS, SECT, QB, QB)
    values = jnp.clip(jax.random.normal(jax.random.fold_in(key, 5), shape, jnp.float32), -4.0, 4.0)
    return values.astype(jnp.bfloat16)


def draw_left_ops(key, part):
    shape = (SEGS, TERMS, SECT, QB, QB)
    blocks = dominant_blocks(jax.random.fold_in(key, 11), shape, 2.0, 6.0, 2.0, False)
    return blocks.astype(jnp.bfloat16)


def draw_right_ops(key, part):
    shape = (SEGS, TERMS, SECT, QB, QB)
    blocks = dominant_blocks(jax.random.fold_in(key, 23), shape, 2.0, 6.0, 2.0, False)
    return blocks.astype(jnp.bfloat16)


def place_ends(values, stream_key, low, largest):
    longest = values.shape.index(max(values.shape))
    spots = []
    for shift in (0, 1):
        where = [jax.random.randint(jax.random.fold_in(stream_key, axis), (), 0, length) for axis, length in enumerate(values.shape)]
        where[longest] = (where[longest] + shift) % values.shape[longest]
        spots.append(tuple(where))
    return values.at[spots[0]].set(low).at[spots[1]].set(largest)


def setup_inputs(seed: int = 0) -> dict:
    splits = jax.random.split(jax.random.key(seed), 6)
    return {
        "psi_start": draw_psi_start(jax.random.fold_in(splits[5], 71), 0),
        "left_ops": draw_left_ops(jax.random.fold_in(splits[5], 71), 0),
        "right_ops": draw_right_ops(jax.random.fold_in(splits[5], 71), 0),
        "shifts": place_ends(jax.random.randint(splits[3], (SEGS, TERMS), 0, SECT), jax.random.fold_in(splits[3], 1), 0, SECT - 1).astype(jnp.int32),
        "active": place_ends((jax.random.randint(splits[4], (SEGS, TERMS, SECT), 0, 2) < 1).astype(jnp.int32), jax.random.fold_in(splits[4], 1), 0, 1),
    }


precise = lax.Precision.HIGHEST
step_size = 0.3

def blockmul(left, right):
    return jnp.einsum('sij,sjl->sil', left, right, precision=precise)

def gram_blocks(piece):
    wide = piece.astype(jnp.float32)
    return jnp.einsum('sji,sjl->sil', wide, wide, precision=precise)

def term_parts(state_low, left_k, right_k):
    half = jnp.einsum('sij,sjl->sil', left_k.astype(jnp.float32), state_low.astype(jnp.float32), precision=precise).astype(jnp.bfloat16)
    return jnp.einsum('sil,sml->sim', half.astype(jnp.float32), right_k.astype(jnp.float32), precision=precise)

def term_sum(state_low, lefts, rights, weights, shift_list):

    def add_term(running, items):
        left_k, right_k, weight_k, shift_k = items
        placed = weight_k[:, None, None] * term_parts(state_low, left_k, right_k)
        return (running + jnp.roll(placed, shift_k, axis=0), None)
    start_sum = jnp.zeros((SECT, QB, QB), jnp.float32)
    summed, _ = lax.scan(add_term, start_sum, (lefts, rights, weights, shift_list))
    return summed * (1.0 / TERMS)

def term_values(state_low, lefts, rights, weights, shift_list):
    wide_low = state_low.astype(jnp.float32)

    def one_term(carried, items):
        left_k, right_k, weight_k, shift_k = items
        target = jnp.roll(wide_low, -shift_k, axis=0)
        per_block = lax.optimization_barrier(jnp.sum(term_parts(state_low, left_k, right_k) * target, axis=(1, 2)))
        return (carried, jnp.sum(weight_k * per_block) * (1.0 / (SECT * QB * QB)))
    _, values = lax.scan(one_term, jnp.zeros((), jnp.float32), (lefts, rights, weights, shift_list))
    return values

def reference(psi_start, left_ops, right_ops, shifts, active):
    count = float(SECT * QB * QB)
    states = [psi_start[seg_index].astype(jnp.float32) for seg_index in range(N_SEG)]
    for sweep_index in range(ITERS):
        lows = [current.astype(jnp.bfloat16) for current in states]
        updated = []
        for seg_index in range(N_SEG):
            current = states[seg_index]
            env = jnp.zeros((SECT, QB, QB), jnp.float32)
            if seg_index > 0:
                env = env + gram_blocks(lows[seg_index - 1])
            if seg_index < N_SEG - 1:
                env = env + gram_blocks(lows[seg_index + 1])
            weights = active[seg_index].astype(jnp.float32)
            applied = term_sum(lows[seg_index], left_ops[seg_index], right_ops[seg_index], weights, shifts[seg_index]) + blockmul(current, env) * (0.5 / QB)
            rho = jnp.sum(current * applied) / jnp.sum(current * current)
            stepped = current - step_size * (applied - rho * current)
            updated.append(stepped * jnp.sqrt(count / jnp.sum(stepped * stepped)))
        states = updated
    finals = [current.astype(jnp.bfloat16) for current in states]
    values = []
    for seg_index in range(N_SEG):
        weights = active[seg_index].astype(jnp.float32)
        values.append(term_values(finals[seg_index], left_ops[seg_index], right_ops[seg_index], weights, shifts[seg_index]))
    return (jnp.stack(finals), jnp.stack(values))
```

```python
import functools

import jax
import jax.numpy as jnp
from jax import lax
from jax.experimental import pallas as pl
from jax.experimental.pallas import tpu as pltpu
from jax.sharding import PartitionSpec as P

ITERS = 3
GROUP = 8
TAIL = 16
STRIP = 64

step_size = 0.3
low_type = jnp.bfloat16
wide_type = jnp.float32
VMEM = pl.BlockSpec(memory_space=pltpu.VMEM)
SMEM = pl.BlockSpec(memory_space=pltpu.SMEM)


def params(megabytes):
    return pltpu.CompilerParams(vmem_limit_bytes=megabytes << 20)


def traded(block, distance):
    route = [(i, i ^ distance) for i in range(lax.axis_size("op"))]
    return lax.ppermute(block, "op", route)


def shifted(block, distance):
    devices = range(lax.axis_size("seg"))
    route = [(i - distance, i) for i in devices if i - distance in devices]
    return lax.ppermute(block, "seg", route)


def gathered(block):
    devices = lax.axis_size("op")
    held = [block] + [None] * (devices - 1)
    for distance in range(devices - 2, 0, -2):
        held[distance] = traded(block, distance)
    held[1] = traded(block, 1)
    for distance in range(2, devices, 2):
        held[distance + 1] = traded(held[distance], 1)
    return held


def plan_kernel(blocks_dev, me_ref, shifts_ref, active_ref, pair_ref, source_ref, target_ref, term_ref, count_ref):
    terms, blocks_all = active_ref.shape
    me = me_ref[0]

    def slot(block):
        return ((block // blocks_dev) ^ me) * blocks_dev + block % blocks_dev

    def one(flat, found):
        term = flat // blocks_all
        block = flat % blocks_all
        target = block + shifts_ref[0, term]
        target = jnp.where(target >= blocks_all, target - blocks_all, target)
        pair_ref[found] = flat
        source_ref[found] = slot(block)
        target_ref[found] = slot(target)
        term_ref[found] = term
        return found + active_ref[term, block]

    found = lax.fori_loop(0, terms * blocks_all, one, 0)
    count_ref[0] = found
    for extra in range(GROUP):
        pair_ref[found + extra] = 0
        source_ref[found + extra] = 0
        target_ref[found + extra] = blocks_all
        term_ref[found + extra] = terms


def make_plan(me, shifts, active, blocks_dev):
    terms, blocks_all = active.shape
    entries = jax.ShapeDtypeStruct((terms * blocks_all + GROUP,), jnp.int32)
    return pl.pallas_call(
        functools.partial(plan_kernel, blocks_dev),
        out_shape=[entries] * 4 + [jax.ShapeDtypeStruct((1,), jnp.int32)],
        in_specs=[SMEM] * 3,
        out_specs=[SMEM] * 5,
    )(me, shifts, active)


def pair_product(index, pair_ref, source_ref, left_ref, right_ref, low_ref):
    pair = pair_ref[index]
    half = jnp.dot(left_ref[pair], low_ref[source_ref[index]], preferred_element_type=wide_type).astype(low_type)
    return lax.dot_general(half, right_ref[pair], (((1,), (1,)), ((), ())), preferred_element_type=wide_type)


def fill_low(first, chunk_refs, own_ref, old_refs, low_ref, fresh_ref, count):
    rows = own_ref.shape[0]
    width = own_ref.shape[1]
    if first:
        for place, chunk_ref in enumerate(chunk_refs):
            blocks = rows // width
            low_ref[place * blocks : (place + 1) * blocks] = chunk_ref[...].reshape(blocks, width, width)
        return
    tails = sum(ref[rows:, :].astype(wide_type) for ref in chunk_refs)

    def total(which):
        return tails[3 * which : 3 * which + 1] + tails[3 * which + 1 : 3 * which + 2] + tails[3 * which + 2 : 3 * which + 3]

    squares, cross, applied_squares = total(0), total(1), total(2)
    rho = cross / squares
    length = squares + step_size * step_size * (applied_squares - rho * cross)
    scale = jnp.sqrt(count / length)
    keep = scale * (1.0 + step_size * rho)
    take = scale * step_size
    for place, chunk_ref in enumerate(chunk_refs):
        source = own_ref if place == 0 else chunk_ref

        def strip(part, carried, place=place, source=source):
            start = pl.multiple_of(part * STRIP, STRIP)
            if len(old_refs) == 1:
                old = old_refs[0][pl.ds(place * rows + start, STRIP), :]
            else:
                old = old_refs[place][pl.ds(start, STRIP), :].astype(wide_type)
            new = keep * old - take * source[pl.ds(start, STRIP), :].astype(wide_type)
            if fresh_ref is not None:
                fresh_ref[pl.ds(place * rows + start, STRIP), :] = new
            low = new.astype(low_type)
            at = place * rows + start
            low_ref[at // width, pl.ds(pl.multiple_of(at % width, STRIP), STRIP), :] = low
            return carried

        lax.fori_loop(0, rows // STRIP, strip, 0, unroll=True)


def apply_kernel(first, devices, olds, count, term_scale, *refs):
    pair_ref, source_ref, target_ref, count_ref, left_ref, right_ref = refs[:6]
    chunk_refs = refs[6 : 6 + devices]
    own_ref = refs[6 + devices]
    old_refs = refs[7 + devices : 7 + devices + olds]
    rest = refs[7 + devices + olds :]
    half = devices // 2
    send_refs, keep_refs = rest[:half], rest[half : 2 * half]
    rest = rest[2 * half :]
    if first:
        fresh_ref = None
    else:
        fresh_ref, own_low_ref, own_wide_ref = rest[:3]
        rest = rest[3:]
    low_ref, sum_ref = rest
    rows, width = own_ref.shape
    blocks = rows // width
    fill_low(first, chunk_refs, own_ref, old_refs, low_ref, fresh_ref, count)
    if not first:
        own_low_ref[...] = low_ref[:blocks].reshape(rows, width)
        own_wide_ref[...] = fresh_ref[:rows, :]
    sum_ref[...] = jnp.zeros_like(sum_ref)

    def group(index, carried):
        products = [
            pair_product(index * GROUP + inner, pair_ref, source_ref, left_ref, right_ref, low_ref)
            for inner in range(GROUP)
        ]
        for inner, product in enumerate(products):
            sum_ref[target_ref[index * GROUP + inner]] += product
        return carried

    lax.fori_loop(0, (count_ref[0] + GROUP - 1) // GROUP, group, 0)
    for place in range(half):
        keep_at = 2 * place * blocks
        keep_refs[place][...] = sum_ref[keep_at : keep_at + blocks].reshape(rows, width) * term_scale
        send_at = keep_at + blocks
        send_refs[place][...] = (sum_ref[send_at : send_at + blocks].reshape(rows, width) * term_scale).astype(low_type)


def apply_terms(plan, lefts, rights, chunks, own, olds, count, term_scale):
    first = not olds
    devices = len(chunks)
    rows, width = own.shape
    total = devices * rows
    pairs, sources, targets, _, found = plan
    outs = [jax.ShapeDtypeStruct((rows, width), low_type)] * (devices // 2)
    outs += [jax.ShapeDtypeStruct((rows, width), wide_type)] * (devices // 2)
    if not first:
        outs += [
            jax.ShapeDtypeStruct((total, width), wide_type),
            jax.ShapeDtypeStruct((rows, width), low_type),
            jax.ShapeDtypeStruct((rows, width), wide_type),
        ]
    pairs_all = lefts.shape[0]
    return pl.pallas_call(
        functools.partial(apply_kernel, first, devices, len(olds), count, term_scale),
        out_shape=outs,
        in_specs=[SMEM] * 4 + [VMEM] * (3 + devices + len(olds)),
        out_specs=[VMEM] * len(outs),
        scratch_shapes=[
            pltpu.VMEM((total // width, width, width), low_type),
            pltpu.VMEM((total // width + 1, width, width), wide_type),
        ],
        compiler_params=params(32),
        cost_estimate=pl.CostEstimate(flops=2 * pairs_all * width**3, bytes_accessed=4 << 20, transcendentals=0),
    )(pairs, sources, targets, found, lefts, rights, *chunks, own, *olds)


def values_kernel(devices, olds, count, *refs):
    pair_ref, source_ref, target_ref, term_ref, count_ref, left_ref, right_ref = refs[:7]
    chunk_refs = refs[7 : 7 + devices]
    own_ref = refs[7 + devices]
    old_refs = refs[8 + devices : 8 + devices + olds]
    state_ref, value_ref, low_ref, sum_ref = refs[8 + devices + olds :]
    rows, width = own_ref.shape
    blocks = rows // width
    fill_low(False, chunk_refs, own_ref, old_refs, low_ref, None, count)
    state_ref[...] = low_ref[:blocks].reshape(rows, width)
    low_ref[devices * blocks] = jnp.zeros((width, width), low_type)
    sum_ref[...] = jnp.zeros_like(sum_ref)

    def group(index, carried):
        products = [
            pair_product(index * GROUP + inner, pair_ref, source_ref, left_ref, right_ref, low_ref)
            for inner in range(GROUP)
        ]
        for inner, product in enumerate(products):
            place = index * GROUP + inner
            target = low_ref[target_ref[place]].astype(wide_type)
            folded = (product * target).reshape(width // 8, 8, width).sum(axis=0)
            sum_ref[term_ref[place]] += folded
        return carried

    lax.fori_loop(0, (count_ref[0] + GROUP - 1) // GROUP, group, 0)
    terms = value_ref.shape[0]
    for term in range(terms):
        value_ref[term : term + 1, :] = jnp.full((1, width), jnp.sum(sum_ref[term]) * (1.0 / count))


def term_values(plan, lefts, rights, chunks, own, olds, count, terms):
    devices = len(chunks)
    rows, width = own.shape
    total = devices * rows
    pairs_all = lefts.shape[0]
    return pl.pallas_call(
        functools.partial(values_kernel, devices, len(olds), count),
        out_shape=[jax.ShapeDtypeStruct((rows, width), low_type), jax.ShapeDtypeStruct((terms, width), wide_type)],
        in_specs=[SMEM] * 5 + [VMEM] * (3 + devices + len(olds)),
        out_specs=[VMEM] * 2,
        scratch_shapes=[
            pltpu.VMEM((total // width + 1, width, width), low_type),
            pltpu.VMEM((terms + 1, 8, width), wide_type),
        ],
        compiler_params=params(32),
        cost_estimate=pl.CostEstimate(flops=2 * pairs_all * width**3, bytes_accessed=4 << 20, transcendentals=0),
    )(*plan, lefts, rights, *chunks, own, *olds)


def coupling_kernel(own_ref, before_ref, after_ref, out_ref):
    rows, width = own_ref.shape
    for block in range(rows // width):
        at = pl.ds(block * width, width)
        gram = sum(
            lax.dot_general(ref[at, :], ref[at, :], (((0,), (0,)), ((), ())), preferred_element_type=wide_type)
            for ref in (before_ref, after_ref)
        )
        out_ref[at, :] = jnp.dot(
            own_ref[at, :], gram, precision=lax.Precision.HIGHEST, preferred_element_type=wide_type
        ) * (0.5 / width)


def coupling(own, before, after):
    rows, width = own.shape
    return pl.pallas_call(
        coupling_kernel,
        out_shape=jax.ShapeDtypeStruct(own.shape, wide_type),
        in_specs=[VMEM] * 3,
        out_specs=VMEM,
        cost_estimate=pl.CostEstimate(flops=16 * rows * width**2, bytes_accessed=rows * width * 12, transcendentals=0),
    )(own, before, after)


def total_kernel(parts, own_ref, coupled_ref, *refs):
    part_refs, (applied_ref, sent_ref) = refs[:parts], refs[parts:]
    rows, width = own_ref.shape
    sums = [jnp.zeros((8, width), wide_type)] * 3
    for start in range(0, rows, STRIP):
        at = pl.ds(start, STRIP)
        applied = coupled_ref[at, :] + sum(ref[at, :].astype(wide_type) for ref in part_refs)
        own = own_ref[at, :].astype(wide_type)
        applied_ref[at, :] = applied
        sent_ref[at, :] = applied.astype(low_type)
        for which, product in enumerate((own * own, own * applied, applied * applied)):
            sums[which] = sums[which] + product.reshape(STRIP // 8, 8, width).sum(axis=0)
    row = lax.broadcasted_iota(jnp.int32, (TAIL, width), 0)
    tail = jnp.zeros((TAIL, width), wide_type)
    for which in range(3):
        rest = jnp.full((TAIL, width), jnp.sum(sums[which]))
        for digit in range(3):
            rounded = rest.astype(low_type).astype(wide_type)
            tail = jnp.where(row == 3 * which + digit, rounded, tail)
            rest = rest - rounded
    sent_ref[rows:, :] = tail.astype(low_type)


def total_applied(own, coupled, parts):
    rows, width = own.shape
    return pl.pallas_call(
        functools.partial(total_kernel, len(parts)),
        out_shape=[jax.ShapeDtypeStruct((rows, width), wide_type), jax.ShapeDtypeStruct((rows + TAIL, width), low_type)],
        in_specs=[VMEM] * (2 + len(parts)),
        out_specs=[VMEM] * 2,
        cost_estimate=pl.CostEstimate(flops=10 * rows * width, bytes_accessed=rows * width * 16, transcendentals=0),
    )(own, coupled, *parts)


def shards(psi_start, left_ops, right_ops, shifts, active):
    devices = lax.axis_size("op")
    terms, blocks_all, width = left_ops.shape[1:4]
    blocks_dev = psi_start.shape[1]
    rows = blocks_dev * width
    count = float(blocks_all * width * width)
    term_scale = 1.0 / (terms * devices)
    lefts = pltpu.with_memory_space_constraint(left_ops.reshape(terms * blocks_all, width, width), pltpu.VMEM)
    rights = pltpu.with_memory_space_constraint(right_ops.reshape(terms * blocks_all, width, width), pltpu.VMEM)
    own_low = psi_start.reshape(rows, width)
    own_wide = own_low
    me = lax.axis_index("op").astype(jnp.int32).reshape(1)
    plan = make_plan(me, shifts, active[0], blocks_dev)
    chunks = gathered(own_low)
    own_source = own_low
    olds = []
    for sweep_index in range(ITERS):
        outs = apply_terms(plan, lefts, rights, chunks, own_source, olds, count, term_scale)
        half = devices // 2
        sends, keeps = outs[:half], outs[half : 2 * half]
        if olds:
            fresh, own_low, own_wide = outs[2 * half :]
            olds = [fresh]
        else:
            olds = chunks
        before, after = shifted(own_low, 1), shifted(own_low, -1)
        parts = [keeps[0]]
        for place in range(half - 1, -1, -1):
            arrived = traded(sends[place], 1)
            if place:
                joined = (keeps[place] + arrived.astype(wide_type)).astype(low_type)
                parts.append(traded(joined, 2 * place))
            else:
                parts.append(arrived)
        coupled = coupling(own_wide.astype(wide_type), before, after)
        own_source, sent = total_applied(own_wide, coupled, parts)
        chunks = gathered(sent)
    state, values = term_values(plan, lefts, rights, chunks, own_source, olds, count, terms)
    return state.reshape(psi_start.shape), values[:, 0].reshape(shifts.shape)


def solution(mesh):
    return jax.shard_map(
        shards,
        mesh=mesh,
        in_specs=(
            P("seg", "op", None, None),
            P("seg", "op", None, None, None),
            P("seg", "op", None, None, None),
            P("seg", "op"),
            P("seg", "op", None),
        ),
        out_specs=(P("seg", "op", None, None), P("seg", "op")),
        check_vma=False,
    )
```

```python
import functools

import jax
import jax.numpy as jnp
from jax import lax
from jax.experimental import pallas as pl
from jax.experimental.pallas import tpu as pltpu
from jax.sharding import PartitionSpec as P

ITERS = 3
GROUP = 8
TAIL = 16
STRIP = 64

step_size = 0.3
low_type = jnp.bfloat16
wide_type = jnp.float32
VMEM = pl.BlockSpec(memory_space=pltpu.VMEM)
SMEM = pl.BlockSpec(memory_space=pltpu.SMEM)


def params(megabytes):
    return pltpu.CompilerParams(vmem_limit_bytes=megabytes << 20)


def pinned(array):
    return pltpu.with_memory_space_constraint(array, pltpu.VMEM)


def kept(shape, dtype):
    return pltpu.VMEM(shape, dtype)


def traded(block, distance):
    route = [(i, i ^ distance) for i in range(lax.axis_size("op"))]
    return lax.ppermute(block, "op", route)


def neighbours(block):
    devices = lax.axis_size("seg")
    found = []
    for first in (0, 1):
        pairs = [(i, i + 1) for i in range(first, devices - 1, 2)]
        found.append(lax.ppermute(block, "seg", pairs + [(j, i) for i, j in pairs]))
    return found


def hop(place):
    return 2 if place == 3 else place & -place


def branches(place, devices):
    return [further for further in range(1, devices) if further ^ hop(further) == place]


def depth(place):
    return 0 if place == 0 else 1 + depth(place ^ hop(place))


def leaves(devices):
    return [place for place in range(1, devices) if not branches(place, devices)]


def gathered(block):
    devices = lax.axis_size("op")
    held = {0: block}
    for place in sorted(range(1, devices), key=depth):
        held[place] = traded(held[place ^ hop(place)], hop(place))
    return [held[place] for place in range(devices)]


def summed(pieces):
    devices = len(pieces)
    came = {place: [] for place in range(devices)}
    for place in sorted(range(1, devices), key=depth, reverse=True):
        piece = pieces[place]
        if came[place]:
            piece = sum((part.astype(wide_type) for part in came[place]), piece).astype(low_type)
        came[place ^ hop(place)].append(traded(piece, hop(place)))
    return [pieces[0], *came[0]]


def plan_kernel(blocks_dev, me_ref, shifts_ref, active_ref, left_hbm, right_hbm, plan_ref, left_ref, turned_ref, right_ref, arrived):
    copies = [
        pltpu.make_async_copy(left_hbm, left_ref, arrived.at[0]),
        pltpu.make_async_copy(right_hbm, right_ref, arrived.at[1]),
    ]
    for copy in copies:
        copy.start()
    terms, blocks_all = active_ref.shape
    room = plan_ref.shape[1]
    mine = me_ref[0] * blocks_dev
    found = 0
    for term in range(terms):
        shift = shifts_ref[0, term]

        def one(block, found, term=term, shift=shift):
            target = block + shift
            target = jnp.where(target >= blocks_all, target - blocks_all, target)
            plan_ref[0, found] = term * blocks_all + block
            plan_ref[1, found] = block ^ mine
            plan_ref[2, found] = target ^ mine
            plan_ref[3, found] = term
            return found + active_ref[term, block]

        found = lax.fori_loop(0, blocks_all, one, found, unroll=8)
    for extra in range(GROUP):
        plan_ref[0, found + extra] = 0
        plan_ref[1, found + extra] = 0
        plan_ref[2, found + extra] = blocks_all
        plan_ref[3, found + extra] = terms
    plan_ref[0, room - 1] = found
    for copy in copies:
        copy.wait()

    def turn(index, carried):
        for inner in range(GROUP // 2):
            pair = plan_ref[0, index * (GROUP // 2) + inner]
            turned_ref[pair] = right_ref[pair].T
        return carried

    lax.fori_loop(0, (found + GROUP // 2) // (GROUP // 2), turn, 0)


def make_plan(me, shifts, active, lefts, rights, blocks_dev):
    terms, blocks_all = active.shape
    room = terms * blocks_all + GROUP + 1
    far = pl.BlockSpec(memory_space=pltpu.HBM)
    return pl.pallas_call(
        functools.partial(plan_kernel, blocks_dev),
        out_shape=[
            jax.ShapeDtypeStruct((4, room), jnp.int32),
            kept(lefts.shape, lefts.dtype),
            kept(rights.shape, rights.dtype),
        ],
        in_specs=[SMEM] * 3 + [far] * 2,
        out_specs=[SMEM, VMEM, VMEM],
        scratch_shapes=[pltpu.VMEM(rights.shape, rights.dtype), pltpu.SemaphoreType.DMA((2,))],
        compiler_params=params(8),
        cost_estimate=pl.CostEstimate(flops=0, bytes_accessed=16 << 20, transcendentals=0),
    )(me, shifts, active, *(pltpu.with_memory_space_constraint(array, pltpu.HBM) for array in (lefts, rights)))


def pair_product(index, plan_ref, left_ref, right_ref, low_ref):
    pair = plan_ref[0, index]
    half = jnp.dot(left_ref[pair], low_ref[plan_ref[1, index]], preferred_element_type=wide_type).astype(low_type)
    return jnp.dot(half, right_ref[pair], preferred_element_type=wide_type)


def fill_low(first, chunk_refs, own_ref, old_refs, low_ref, fresh_ref, count):
    rows = own_ref.shape[0]
    width = own_ref.shape[1]
    if first:
        for place, chunk_ref in enumerate(chunk_refs):
            blocks = rows // width
            low_ref[place * blocks : (place + 1) * blocks] = chunk_ref[...].reshape(blocks, width, width)
        return
    tails = sum(ref[rows:, :].astype(wide_type) for ref in chunk_refs)

    def total(which):
        return tails[3 * which : 3 * which + 1] + tails[3 * which + 1 : 3 * which + 2] + tails[3 * which + 2 : 3 * which + 3]

    squares, cross, applied_squares = total(0), total(1), total(2)
    rho = cross / squares
    length = squares + step_size * step_size * (applied_squares - rho * cross)
    scale = jnp.sqrt(count / length)
    keep = scale * (1.0 + step_size * rho)
    take = scale * step_size
    for place, chunk_ref in enumerate(chunk_refs):
        source = own_ref if place == 0 else chunk_ref

        def strip(part, carried, place=place, source=source):
            start = pl.multiple_of(part * STRIP, STRIP)
            if len(old_refs) == 1:
                old = old_refs[0][pl.ds(place * rows + start, STRIP), :]
            else:
                old = old_refs[place][pl.ds(start, STRIP), :].astype(wide_type)
            new = keep * old - take * source[pl.ds(start, STRIP), :].astype(wide_type)
            if fresh_ref is not None:
                fresh_ref[pl.ds(place * rows + start, STRIP), :] = new
            low = new.astype(low_type)
            at = place * rows + start
            low_ref[at // width, pl.ds(pl.multiple_of(at % width, STRIP), STRIP), :] = low
            return carried

        lax.fori_loop(0, rows // STRIP, strip, 0, unroll=True)


def apply_kernel(first, devices, olds, count, term_scale, *refs):
    plan_ref, left_ref, right_ref = refs[:3]
    chunk_refs = refs[3 : 3 + devices][::-1]
    own_ref = refs[3 + devices]
    old_refs = refs[4 + devices : 4 + devices + olds]
    rest = refs[4 + devices + olds :]
    piece_refs, rest = rest[:devices], rest[devices:]
    if first:
        fresh_ref = None
    else:
        fresh_ref, own_low_ref, own_wide_ref = rest[:3]
        rest = rest[3:]
    low_ref, sum_ref = rest
    rows, width = own_ref.shape
    blocks = rows // width
    fill_low(first, chunk_refs, own_ref, old_refs, low_ref, fresh_ref, count)
    if not first:
        own_low_ref[...] = low_ref[:blocks].reshape(rows, width)
        own_wide_ref[...] = fresh_ref[:rows, :]
    sum_ref[...] = jnp.zeros_like(sum_ref)

    def group(index, carried):
        products = [
            pair_product(index * GROUP + inner, plan_ref, left_ref, right_ref, low_ref)
            for inner in range(GROUP)
        ]
        for inner, product in enumerate(products):
            sum_ref[plan_ref[2, index * GROUP + inner]] += product
        return carried

    lax.fori_loop(0, (plan_ref[0, plan_ref.shape[1] - 1] + GROUP - 1) // GROUP, group, 0)
    for place, piece_ref in enumerate(piece_refs):
        piece = sum_ref[place * blocks : (place + 1) * blocks].reshape(rows, width) * term_scale
        piece_ref[...] = piece.astype(piece_ref.dtype)


def apply_terms(plan, lefts, rights, chunks, own, olds, count, term_scale):
    first = not olds
    devices = len(chunks)
    rows, width = own.shape
    total = devices * rows
    sent = leaves(devices)
    outs = [kept((rows, width), low_type if place in sent else wide_type) for place in range(devices)]
    if not first:
        outs += [kept((total, width), wide_type), kept((rows, width), low_type), kept((rows, width), wide_type)]
    pairs_all = lefts.shape[0]
    return pl.pallas_call(
        functools.partial(apply_kernel, first, devices, len(olds), count, term_scale),
        out_shape=outs,
        in_specs=[SMEM] + [VMEM] * (3 + devices + len(olds)),
        out_specs=[VMEM] * len(outs),
        scratch_shapes=[
            pltpu.VMEM((total // width, width, width), low_type),
            pltpu.VMEM((total // width + 1, width, width), wide_type),
        ],
        compiler_params=params(12),
        cost_estimate=pl.CostEstimate(flops=2 * pairs_all * width**3, bytes_accessed=4 << 20, transcendentals=0),
    )(plan, *map(pinned, (lefts, rights, *chunks[::-1], own, *olds)))


def values_kernel(devices, olds, count, *refs):
    plan_ref, left_ref, right_ref = refs[:3]
    chunk_refs = refs[3 : 3 + devices][::-1]
    own_ref = refs[3 + devices]
    old_refs = refs[4 + devices : 4 + devices + olds]
    state_ref, value_ref, low_ref, sum_ref = refs[4 + devices + olds :]
    rows, width = own_ref.shape
    blocks = rows // width
    fill_low(False, chunk_refs, own_ref, old_refs, low_ref, None, count)
    state_ref[...] = low_ref[:blocks].reshape(rows, width)
    low_ref[devices * blocks] = jnp.zeros((width, width), low_type)
    sum_ref[...] = jnp.zeros_like(sum_ref)

    def group(index, carried):
        products = [
            pair_product(index * GROUP + inner, plan_ref, left_ref, right_ref, low_ref)
            for inner in range(GROUP)
        ]
        for inner, product in enumerate(products):
            place = index * GROUP + inner
            target = low_ref[plan_ref[2, place]].astype(wide_type)
            folded = (product * target).reshape(width // 8, 8, width).sum(axis=0)
            sum_ref[plan_ref[3, place]] += folded
        return carried

    lax.fori_loop(0, (plan_ref[0, plan_ref.shape[1] - 1] + GROUP - 1) // GROUP, group, 0)
    terms = value_ref.shape[0]
    for term in range(terms):
        value_ref[term : term + 1, :] = jnp.full((1, width), jnp.sum(sum_ref[term]) * (1.0 / count))


def term_values(plan, lefts, rights, chunks, own, olds, count, terms):
    devices = len(chunks)
    rows, width = own.shape
    total = devices * rows
    pairs_all = lefts.shape[0]
    return pl.pallas_call(
        functools.partial(values_kernel, devices, len(olds), count),
        out_shape=[jax.ShapeDtypeStruct((rows, width), low_type), jax.ShapeDtypeStruct((terms, width), wide_type)],
        in_specs=[SMEM] + [VMEM] * (3 + devices + len(olds)),
        out_specs=[VMEM] * 2,
        scratch_shapes=[
            pltpu.VMEM((total // width + 1, width, width), low_type),
            pltpu.VMEM((terms + 1, 8, width), wide_type),
        ],
        compiler_params=params(12),
        cost_estimate=pl.CostEstimate(flops=2 * pairs_all * width**3, bytes_accessed=4 << 20, transcendentals=0),
    )(plan, *map(pinned, (lefts, rights, *chunks[::-1], own, *olds)))


def coupling_kernel(own_ref, before_ref, after_ref, out_ref):
    rows, width = own_ref.shape
    for block in range(rows // width):
        at = pl.ds(block * width, width)
        gram = sum(
            lax.dot_general(ref[at, :], ref[at, :], (((0,), (0,)), ((), ())), preferred_element_type=wide_type)
            for ref in (before_ref, after_ref)
        )
        out_ref[at, :] = jnp.dot(
            own_ref[at, :].astype(wide_type), gram, precision=lax.Precision.HIGHEST, preferred_element_type=wide_type
        ) * (0.5 / width)


def coupling(own, before, after):
    rows, width = own.shape
    return pl.pallas_call(
        coupling_kernel,
        out_shape=kept(own.shape, wide_type),
        in_specs=[VMEM] * 3,
        out_specs=VMEM,
        compiler_params=params(4),
        cost_estimate=pl.CostEstimate(flops=0, bytes_accessed=0, transcendentals=0),
    )(*map(pinned, (own, before, after)))


def parts_kernel(*refs):
    *part_refs, out_ref = refs
    for start in range(0, out_ref.shape[0], STRIP):
        at = pl.ds(start, STRIP)
        out_ref[at, :] = sum(ref[at, :].astype(wide_type) for ref in part_refs)


def added(parts):
    shape = parts[0].shape
    return pl.pallas_call(
        parts_kernel,
        out_shape=kept(shape, wide_type),
        in_specs=[VMEM] * len(parts),
        out_specs=VMEM,
        compiler_params=params(4),
        cost_estimate=pl.CostEstimate(flops=1 << 32, bytes_accessed=1 << 24, transcendentals=0),
    )(*map(pinned, parts))


def total_kernel(own_ref, coupled_ref, part_ref, applied_ref, sent_ref):
    rows, width = own_ref.shape
    sums = [jnp.zeros((8, width), wide_type)] * 3
    for start in range(0, rows, STRIP):
        at = pl.ds(start, STRIP)
        applied = coupled_ref[at, :] + part_ref[at, :]
        own = own_ref[at, :].astype(wide_type)
        applied_ref[at, :] = applied
        sent_ref[at, :] = applied.astype(low_type)
        for which, product in enumerate((own * own, own * applied, applied * applied)):
            sums[which] = sums[which] + product.reshape(STRIP // 8, 8, width).sum(axis=0)
    row = lax.broadcasted_iota(jnp.int32, (TAIL, width), 0)
    tail = jnp.zeros((TAIL, width), wide_type)
    for which in range(3):
        rest = jnp.full((TAIL, width), jnp.sum(sums[which]))
        for digit in range(3):
            rounded = rest.astype(low_type).astype(wide_type)
            tail = jnp.where(row == 3 * which + digit, rounded, tail)
            rest = rest - rounded
    sent_ref[rows:, :] = tail.astype(low_type)


def total_applied(own, coupled, part):
    rows, width = own.shape
    return pl.pallas_call(
        total_kernel,
        out_shape=[kept((rows, width), wide_type), kept((rows + TAIL, width), low_type)],
        in_specs=[VMEM] * 3,
        out_specs=[VMEM] * 2,
        compiler_params=params(4),
        cost_estimate=pl.CostEstimate(flops=10 * rows * width, bytes_accessed=rows * width * 16, transcendentals=0),
    )(*map(pinned, (own, coupled, part)))


def shards(psi_start, left_ops, right_ops, shifts, active):
    devices = lax.axis_size("op")
    terms, blocks_all, width = left_ops.shape[1:4]
    blocks_dev = psi_start.shape[1]
    rows = blocks_dev * width
    count = float(blocks_all * width * width)
    term_scale = 1.0 / (terms * devices)
    own_low = psi_start.reshape(rows, width)
    own_wide = own_low
    me = lax.axis_index("op").astype(jnp.int32).reshape(1)
    chunks = gathered(own_low)
    lefts = left_ops.reshape(terms * blocks_all, width, width)
    rights = right_ops.reshape(terms * blocks_all, width, width)
    plan, lefts, rights = make_plan(me, shifts, active[0], lefts, rights, blocks_dev)
    own_source = own_low
    olds = []
    for sweep_index in range(ITERS):
        outs = apply_terms(plan, lefts, rights, chunks, own_source, olds, count, term_scale)
        pieces = outs[:devices]
        if olds:
            fresh, own_low, own_wide = outs[devices:]
            olds = [fresh]
        else:
            olds = chunks
        parts = summed(pieces)
        own_low, _ = lax.optimization_barrier((own_low, parts[1]))
        coupled = coupling(own_wide, *neighbours(own_low))
        own_source, sent = total_applied(own_wide, coupled, added(parts))
        chunks = gathered(sent)
    state, values = term_values(plan, lefts, rights, chunks, own_source, olds, count, terms)
    return state.reshape(psi_start.shape), values[:, 0].reshape(shifts.shape)


def solution(mesh):
    return jax.shard_map(
        shards,
        mesh=mesh,
        in_specs=(
            P("seg", "op", None, None),
            P("seg", "op", None, None, None),
            P("seg", "op", None, None, None),
            P("seg", "op"),
            P("seg", "op", None),
        ),
        out_specs=(P("seg", "op", None, None), P("seg", "op")),
        check_vma=False,
    )
```

```python
import functools

import jax
import jax.numpy as jnp
from jax import lax
from jax.experimental import pallas as pl
from jax.experimental.pallas import tpu as pltpu
from jax.sharding import PartitionSpec as P

ITERS = 3
GROUP = 8
TAIL = 16
STRIP = 64
GATHER_BY = {7: 2}
GATHER_AFTER = {3: (1,), 6: (2,)}
SUM_AFTER = {3: (7,)}

step_size = 0.3
low_type = jnp.bfloat16
wide_type = jnp.float32
VMEM = pl.BlockSpec(memory_space=pltpu.VMEM)
SMEM = pl.BlockSpec(memory_space=pltpu.SMEM)


def params(megabytes):
    return pltpu.CompilerParams(vmem_limit_bytes=megabytes << 20)


def pinned(array):
    return pltpu.with_memory_space_constraint(array, pltpu.VMEM)


def kept(shape, dtype):
    return pltpu.VMEM(shape, dtype)


def traded(block, distance):
    route = [(i, i ^ distance) for i in range(lax.axis_size("op"))]
    return lax.ppermute(block, "op", route)


def neighbours(block):
    devices = lax.axis_size("seg")
    found = []
    for first in (0, 1):
        pairs = [(i, i + 1) for i in range(first, devices - 1, 2)]
        found.append(lax.ppermute(block, "seg", pairs + [(j, i) for i, j in pairs]))
    return found


def hop(place, special={}):
    return special.get(place, place & -place)


def depth(place):
    return place.bit_count()


def after(array, others):
    return lax.optimization_barrier((array, *others))[0] if others else array


def gathered(block, meanwhile=()):
    devices = lax.axis_size("op")
    held = {0: block}
    for place in sorted(range(1, devices), key=depth):
        source = held[place ^ hop(place, GATHER_BY)]
        others = [held[other] for other in GATHER_AFTER.get(place, ())]
        if place == 3:
            others += list(meanwhile)
        source = after(source, others)
        held[place] = traded(source, hop(place, GATHER_BY))
    return [held[place] for place in range(devices)]


def summed(pieces):
    devices = len(pieces)
    came = {place: [] for place in range(devices)}
    arrived = {}
    for place in sorted(range(1, devices), key=lambda place: (depth(place), place), reverse=True):
        piece = pieces[place]
        step = hop(place)
        if came[place]:
            piece = sum((part.astype(wide_type) for part in came[place]), piece.astype(wide_type)).astype(low_type)
        piece = after(piece, [arrived[other] for other in SUM_AFTER.get(place, ())])
        arrived[place] = traded(piece, step)
        came[place ^ step].append(arrived[place])
    return [pieces[0], *came[0][::-1]], arrived


def plan_kernel(blocks_dev, me_ref, shifts_ref, active_ref, left_hbm, right_hbm, plan_ref, left_ref, turned_ref, right_ref, arrived):
    copies = [
        pltpu.make_async_copy(left_hbm, left_ref, arrived.at[0]),
        pltpu.make_async_copy(right_hbm, right_ref, arrived.at[1]),
    ]
    for copy in copies:
        copy.start()
    terms, blocks_all = active_ref.shape
    room = plan_ref.shape[1] // 2
    mine = me_ref[0] * blocks_dev
    bits = blocks_dev.bit_length() - 1
    last = blocks_all // blocks_dev - 1
    found = (0, 0)
    for term in range(terms):
        shift = shifts_ref[0, term]

        def one(block, found, term=term, shift=shift):
            target = block + shift
            target = jnp.where(target >= blocks_all, target - blocks_all, target) ^ mine
            ahead = ((target >> bits) == last).astype(jnp.int32)
            at = jnp.where(ahead == 1, found[0], room + found[1])
            plan_ref[0, at] = term * blocks_all + block
            plan_ref[1, at] = block ^ mine
            plan_ref[2, at] = target - ahead * (last * blocks_dev)
            plan_ref[3, at] = term
            plan_ref[4, at] = target
            is_active = active_ref[term, block]
            counted = is_active & ahead
            return found[0] + counted, found[1] + is_active - counted

        found = lax.fori_loop(0, blocks_all, one, found, unroll=8)
    for side in range(2):
        for extra in range(GROUP):
            at = side * room + found[side] + extra
            plan_ref[0, at] = 0
            plan_ref[1, at] = 0
            plan_ref[2, at] = (1, last)[side] * blocks_dev
            plan_ref[3, at] = terms
            plan_ref[4, at] = blocks_all
        plan_ref[0, (side + 1) * room - 1] = found[side]
    for copy in copies:
        copy.wait()

    for side in range(2):

        def turn(index, carried, side=side):
            for inner in range(GROUP // 2):
                pair = plan_ref[0, side * room + index * (GROUP // 2) + inner]
                turned_ref[pair] = right_ref[pair].T
            return carried

        lax.fori_loop(0, (found[side] + GROUP // 2) // (GROUP // 2), turn, 0)


def make_plan(me, shifts, active, lefts, rights, blocks_dev):
    terms, blocks_all = active.shape
    room = terms * blocks_all + GROUP + 1
    far = pl.BlockSpec(memory_space=pltpu.HBM)
    return pl.pallas_call(
        functools.partial(plan_kernel, blocks_dev),
        out_shape=[
            jax.ShapeDtypeStruct((5, 2 * room), jnp.int32),
            kept(lefts.shape, lefts.dtype),
            kept(rights.shape, rights.dtype),
        ],
        in_specs=[SMEM] * 3 + [far] * 2,
        out_specs=[SMEM, VMEM, VMEM],
        scratch_shapes=[pltpu.VMEM(rights.shape, rights.dtype), pltpu.SemaphoreType.DMA((2,))],
        compiler_params=params(8),
        cost_estimate=pl.CostEstimate(flops=0, bytes_accessed=16 << 20, transcendentals=0),
    )(me, shifts, active, *(pltpu.with_memory_space_constraint(array, pltpu.HBM) for array in (lefts, rights)))


def pair_product(index, plan_ref, left_ref, right_ref, low_ref):
    pair = plan_ref[0, index]
    half = jnp.dot(left_ref[pair], low_ref[plan_ref[1, index]], preferred_element_type=wide_type).astype(low_type)
    return jnp.dot(half, right_ref[pair], preferred_element_type=wide_type)


def fill_low(first, chunk_refs, own_ref, old_refs, low_ref, fresh_ref, count):
    rows = own_ref.shape[0]
    width = own_ref.shape[1]
    if first:
        for place, chunk_ref in enumerate(chunk_refs):
            blocks = rows // width
            low_ref[place * blocks : (place + 1) * blocks] = chunk_ref[...].reshape(blocks, width, width)
        return
    tails = sum(ref[rows:, :].astype(wide_type) for ref in chunk_refs)

    def total(which):
        return tails[3 * which : 3 * which + 1] + tails[3 * which + 1 : 3 * which + 2] + tails[3 * which + 2 : 3 * which + 3]

    squares, cross, applied_squares = total(0), total(1), total(2)
    rho = cross / squares
    length = squares + step_size * step_size * (applied_squares - rho * cross)
    scale = jnp.sqrt(count / length)
    keep = scale * (1.0 + step_size * rho)
    take = scale * step_size
    for place, chunk_ref in enumerate(chunk_refs):
        source = own_ref if place == 0 else chunk_ref

        def strip(part, carried, place=place, source=source):
            start = pl.multiple_of(part * STRIP, STRIP)
            if len(old_refs) == 1:
                old = old_refs[0][pl.ds(place * rows + start, STRIP), :]
            else:
                old = old_refs[place][pl.ds(start, STRIP), :].astype(wide_type)
            new = keep * old - take * source[pl.ds(start, STRIP), :].astype(wide_type)
            if fresh_ref is not None:
                fresh_ref[pl.ds(place * rows + start, STRIP), :] = new
            low = new.astype(low_type)
            at = place * rows + start
            low_ref[at // width, pl.ds(pl.multiple_of(at % width, STRIP), STRIP), :] = low
            return carried

        lax.fori_loop(0, rows // STRIP, strip, 0, unroll=True)


def grouped(side, plan_ref, left_ref, right_ref, low_ref, take):
    room = plan_ref.shape[1] // 2

    def group(index, carried):
        first = side * room + index * GROUP
        products = [pair_product(first + inner, plan_ref, left_ref, right_ref, low_ref) for inner in range(GROUP)]
        for inner, product in enumerate(products):
            take(first + inner, product)
        return carried

    lax.fori_loop(0, (plan_ref[0, (side + 1) * room - 1] + GROUP - 1) // GROUP, group, 0)


def add_terms(side, term_scale, plan_ref, left_ref, right_ref, low_ref, piece_refs, sum_ref):
    rows, width = piece_refs[0].shape
    blocks = rows // width
    sum_ref[...] = jnp.zeros_like(sum_ref)

    def take(place, product):
        sum_ref[plan_ref[2, place]] += product

    grouped(side, plan_ref, left_ref, right_ref, low_ref, take)
    for place, piece_ref in enumerate(piece_refs):
        piece = sum_ref[place * blocks : (place + 1) * blocks].reshape(rows, width) * term_scale
        piece_ref[...] = piece.astype(piece_ref.dtype)


def far_kernel(first, devices, olds, count, term_scale, *refs):
    plan_ref, left_ref, right_ref = refs[:3]
    chunk_refs = refs[3 : 3 + devices]
    own_ref = refs[3 + devices]
    old_refs = refs[4 + devices : 4 + devices + olds]
    piece_ref, low_ref, *rest, sum_ref = refs[4 + devices + olds :]
    rows, width = own_ref.shape
    fresh_ref = None if first else rest[0]
    fill_low(first, chunk_refs, own_ref, old_refs, low_ref, fresh_ref, count)
    if not first:
        own_low_ref, own_wide_ref = rest[1:]
        own_low_ref[...] = low_ref[: rows // width].reshape(rows, width)
        own_wide_ref[...] = fresh_ref[:rows, :]
    add_terms(0, term_scale, plan_ref, left_ref, right_ref, low_ref, [piece_ref], sum_ref)


def near_kernel(term_scale, plan_ref, left_ref, right_ref, low_ref, *refs):
    *piece_refs, sum_ref = refs
    add_terms(1, term_scale, plan_ref, left_ref, right_ref, low_ref, piece_refs, sum_ref)


def apply_terms(plan, lefts, rights, chunks, own, olds, count, term_scale):
    first = not olds
    devices = len(chunks)
    rows, width = own.shape
    blocks = rows // width
    total = devices * rows
    blocks_all = total // width
    outs = [kept((rows, width), low_type), kept((blocks_all, width, width), low_type)]
    if not first:
        outs += [kept((total, width), wide_type), kept((rows, width), low_type), kept((rows, width), wide_type)]
    cost = pl.CostEstimate(flops=lefts.shape[0] * width**3, bytes_accessed=4 << 20, transcendentals=0)
    sent = pl.pallas_call(
        functools.partial(far_kernel, first, devices, len(olds), count, term_scale),
        out_shape=outs,
        in_specs=[SMEM] + [VMEM] * (3 + devices + len(olds)),
        out_specs=[VMEM] * len(outs),
        scratch_shapes=[pltpu.VMEM((blocks + 1, width, width), wide_type)],
        compiler_params=params(12),
        cost_estimate=cost,
    )(plan, *map(pinned, (lefts, rights, *chunks, own, *olds)))
    last, low, *current = sent
    pieces = pl.pallas_call(
        functools.partial(near_kernel, term_scale),
        out_shape=[kept((rows, width), low_type if place % 2 else wide_type) for place in range(devices - 1)],
        in_specs=[SMEM] + [VMEM] * 3,
        out_specs=[VMEM] * (devices - 1),
        scratch_shapes=[pltpu.VMEM((blocks_all - blocks + 1, width, width), wide_type)],
        compiler_params=params(12),
        cost_estimate=cost,
    )(plan, *map(pinned, (lefts, rights, low)))
    return [*pieces, last], current


def values_kernel(devices, olds, count, *refs):
    plan_ref, left_ref, right_ref = refs[:3]
    chunk_refs = refs[3 : 3 + devices]
    own_ref = refs[3 + devices]
    old_refs = refs[4 + devices : 4 + devices + olds]
    state_ref, value_ref, low_ref, sum_ref = refs[4 + devices + olds :]
    rows, width = own_ref.shape
    blocks = rows // width
    fill_low(False, chunk_refs, own_ref, old_refs, low_ref, None, count)
    state_ref[...] = low_ref[:blocks].reshape(rows, width)
    low_ref[devices * blocks] = jnp.zeros((width, width), low_type)
    sum_ref[...] = jnp.zeros_like(sum_ref)

    def take(place, product):
        target = low_ref[plan_ref[4, place]].astype(wide_type)
        folded = (product * target).reshape(width // 8, 8, width).sum(axis=0)
        sum_ref[plan_ref[3, place]] += folded

    for side in range(2):
        grouped(side, plan_ref, left_ref, right_ref, low_ref, take)
    terms = value_ref.shape[0]
    for term in range(terms):
        value_ref[term : term + 1, :] = jnp.full((1, width), jnp.sum(sum_ref[term]) * (1.0 / count))


def term_values(plan, lefts, rights, chunks, own, olds, count, terms):
    devices = len(chunks)
    rows, width = own.shape
    total = devices * rows
    pairs_all = lefts.shape[0]
    return pl.pallas_call(
        functools.partial(values_kernel, devices, len(olds), count),
        out_shape=[jax.ShapeDtypeStruct((rows, width), low_type), jax.ShapeDtypeStruct((terms, width), wide_type)],
        in_specs=[SMEM] + [VMEM] * (3 + devices + len(olds)),
        out_specs=[VMEM] * 2,
        scratch_shapes=[
            pltpu.VMEM((total // width + 1, width, width), low_type),
            pltpu.VMEM((terms + 1, 8, width), wide_type),
        ],
        compiler_params=params(12),
        cost_estimate=pl.CostEstimate(flops=2 * pairs_all * width**3, bytes_accessed=4 << 20, transcendentals=0),
    )(plan, *map(pinned, (lefts, rights, *chunks, own, *olds)))


def coupling_kernel(own_ref, before_ref, after_ref, out_ref):
    rows, width = own_ref.shape
    for block in range(rows // width):
        at = pl.ds(block * width, width)
        gram = sum(
            lax.dot_general(ref[at, :], ref[at, :], (((0,), (0,)), ((), ())), preferred_element_type=wide_type)
            for ref in (before_ref, after_ref)
        )
        out_ref[at, :] = jnp.dot(
            own_ref[at, :].astype(wide_type), gram, precision=lax.Precision.HIGHEST, preferred_element_type=wide_type
        ) * (0.5 / width)


def coupling(own, before, after):
    rows, width = own.shape
    return pl.pallas_call(
        coupling_kernel,
        out_shape=kept(own.shape, wide_type),
        in_specs=[VMEM] * 3,
        out_specs=VMEM,
        compiler_params=params(4),
        cost_estimate=pl.CostEstimate(flops=0, bytes_accessed=0, transcendentals=0),
    )(*map(pinned, (own, before, after)))


def parts_kernel(*refs):
    *part_refs, out_ref = refs
    for start in range(0, out_ref.shape[0], STRIP):
        at = pl.ds(start, STRIP)
        out_ref[at, :] = sum(ref[at, :].astype(wide_type) for ref in part_refs)


def added(parts):
    shape = parts[0].shape
    return pl.pallas_call(
        parts_kernel,
        out_shape=kept(shape, wide_type),
        in_specs=[VMEM] * len(parts),
        out_specs=VMEM,
        compiler_params=params(4),
        cost_estimate=pl.CostEstimate(flops=1 << 37, bytes_accessed=1 << 24, transcendentals=0),
    )(*map(pinned, parts))


def total_kernel(own_ref, coupled_ref, part_ref, applied_ref, sent_ref):
    rows, width = own_ref.shape
    sums = [jnp.zeros((8, width), wide_type)] * 3
    for start in range(0, rows, STRIP):
        at = pl.ds(start, STRIP)
        applied = coupled_ref[at, :] + part_ref[at, :]
        own = own_ref[at, :].astype(wide_type)
        applied_ref[at, :] = applied
        sent_ref[at, :] = applied.astype(low_type)
        for which, product in enumerate((own * own, own * applied, applied * applied)):
            sums[which] = sums[which] + product.reshape(STRIP // 8, 8, width).sum(axis=0)
    row = lax.broadcasted_iota(jnp.int32, (TAIL, width), 0)
    tail = jnp.zeros((TAIL, width), wide_type)
    for which in range(3):
        rest = jnp.full((TAIL, width), jnp.sum(sums[which]))
        for digit in range(3):
            rounded = rest.astype(low_type).astype(wide_type)
            tail = jnp.where(row == 3 * which + digit, rounded, tail)
            rest = rest - rounded
    sent_ref[rows:, :] = tail.astype(low_type)


def total_applied(own, coupled, part):
    rows, width = own.shape
    return pl.pallas_call(
        total_kernel,
        out_shape=[kept((rows, width), wide_type), kept((rows + TAIL, width), low_type)],
        in_specs=[VMEM] * 3,
        out_specs=[VMEM] * 2,
        compiler_params=params(4),
        cost_estimate=pl.CostEstimate(flops=10 * rows * width, bytes_accessed=rows * width * 16, transcendentals=0),
    )(*map(pinned, (own, coupled, part)))


def shards(psi_start, left_ops, right_ops, shifts, active):
    devices = lax.axis_size("op")
    terms, blocks_all, width = left_ops.shape[1:4]
    blocks_dev = psi_start.shape[1]
    rows = blocks_dev * width
    count = float(blocks_all * width * width)
    term_scale = 1.0 / (terms * devices)
    own_low = psi_start.reshape(rows, width)
    own_wide = own_low
    me = lax.axis_index("op").astype(jnp.int32).reshape(1)
    lefts = left_ops.reshape(terms * blocks_all, width, width)
    rights = right_ops.reshape(terms * blocks_all, width, width)
    plan, lefts, rights = make_plan(me, shifts, active[0], lefts, rights, blocks_dev)
    chunks = gathered(own_low, [plan])
    own_source = own_low
    olds = []
    for sweep_index in range(ITERS):
        pieces, current = apply_terms(plan, lefts, rights, chunks, own_source, olds, count, term_scale)
        if olds:
            fresh, own_low, own_wide = current
            olds = [fresh]
        else:
            olds = chunks
        parts, arrived = summed(pieces)
        around = neighbours(after(own_low, [arrived[6]]))
        coupled = coupling(own_wide, *around)
        own_source, sent = total_applied(own_wide, coupled, added(parts))
        chunks = gathered(sent)
    state, values = term_values(plan, lefts, rights, chunks, own_source, olds, count, terms)
    return state.reshape(psi_start.shape), values[:, 0].reshape(shifts.shape)


def solution(mesh):
    return jax.shard_map(
        shards,
        mesh=mesh,
        in_specs=(
            P("seg", "op", None, None),
            P("seg", "op", None, None, None),
            P("seg", "op", None, None, None),
            P("seg", "op"),
            P("seg", "op", None),
        ),
        out_specs=(P("seg", "op", None, None), P("seg", "op")),
        check_vma=False,
    )
```

```python
import functools

import jax
import jax.numpy as jnp
from jax import lax
from jax.experimental import pallas as pl
from jax.experimental.pallas import tpu as pltpu
from jax.sharding import PartitionSpec as P

ITERS = 3
GROUP = 8
TAIL = 16
STRIP = 64
GATHER_BY = {7: 2}
GATHER_AFTER = {3: (1,), 6: (2,)}
SUM_AFTER = {3: (7,)}

step_size = 0.3
low_type = jnp.bfloat16
wide_type = jnp.float32
VMEM = pl.BlockSpec(memory_space=pltpu.VMEM)
SMEM = pl.BlockSpec(memory_space=pltpu.SMEM)


def params(megabytes):
    return pltpu.CompilerParams(vmem_limit_bytes=megabytes << 20)


def pinned(array):
    return pltpu.with_memory_space_constraint(array, pltpu.VMEM)


def kept(shape, dtype):
    return pltpu.VMEM(shape, dtype)


def traded(block, distance):
    route = [(i, i ^ distance) for i in range(lax.axis_size("op"))]
    return lax.ppermute(block, "op", route)


def neighbours(block):
    devices = lax.axis_size("seg")
    found = []
    for first in (0, 1):
        pairs = [(i, i + 1) for i in range(first, devices - 1, 2)]
        found.append(lax.ppermute(block, "seg", pairs + [(j, i) for i, j in pairs]))
    return found


def hop(place, special={}):
    return special.get(place, place & -place)


def depth(place):
    return place.bit_count()


def after(array, others):
    return lax.optimization_barrier((array, *others))[0] if others else array


def gathered(block, meanwhile=()):
    devices = lax.axis_size("op")
    held = {0: block}
    for place in sorted(range(1, devices), key=depth):
        source = held[place ^ hop(place, GATHER_BY)]
        others = [held[other] for other in GATHER_AFTER.get(place, ())]
        if place in (5, 6):
            others += list(meanwhile)
        source = after(source, others)
        held[place] = traded(source, hop(place, GATHER_BY))
    return [held[place] for place in range(devices)]


def summed(pieces):
    devices = len(pieces)
    came = {place: [] for place in range(devices)}
    arrived = {}
    for place in sorted(range(1, devices), key=lambda place: (depth(place), place), reverse=True):
        piece = pieces[place]
        step = hop(place)
        if came[place]:
            piece = sum((part.astype(wide_type) for part in came[place]), piece.astype(wide_type)).astype(low_type)
        piece = after(piece, [arrived[other] for other in SUM_AFTER.get(place, ())])
        arrived[place] = traded(piece, step)
        came[place ^ step].append(arrived[place])
    return [pieces[0], *came[0][::-1]], arrived


def plan_kernel(blocks_dev, me_ref, shifts_ref, active_ref, left_hbm, right_hbm, plan_ref, left_ref, right_ref, arrived):
    copies = [
        pltpu.make_async_copy(left_hbm, left_ref, arrived.at[0]),
        pltpu.make_async_copy(right_hbm, right_ref, arrived.at[1]),
    ]
    for copy in copies:
        copy.start()
    terms, blocks_all = active_ref.shape
    room = plan_ref.shape[1] // 2
    mine = me_ref[0] * blocks_dev
    bits = blocks_dev.bit_length() - 1
    last = blocks_all // blocks_dev - 1
    found = (0, 0)
    for term in range(terms):
        shift = shifts_ref[0, term]

        def one(block, found, term=term, shift=shift):
            target = block + shift
            target = jnp.where(target >= blocks_all, target - blocks_all, target) ^ mine
            ahead = ((target >> bits) == last).astype(jnp.int32)
            at = jnp.where(ahead == 1, found[0], room + found[1])
            plan_ref[0, at] = term * blocks_all + block
            plan_ref[1, at] = block ^ mine
            plan_ref[2, at] = target - ahead * (last * blocks_dev)
            plan_ref[3, at] = term
            plan_ref[4, at] = target
            is_active = active_ref[term, block]
            counted = is_active & ahead
            return found[0] + counted, found[1] + is_active - counted

        found = lax.fori_loop(0, blocks_all, one, found, unroll=8)
    for side in range(2):
        for extra in range(GROUP):
            at = side * room + found[side] + extra
            plan_ref[0, at] = 0
            plan_ref[1, at] = 0
            plan_ref[2, at] = (1, last)[side] * blocks_dev
            plan_ref[3, at] = terms
            plan_ref[4, at] = blocks_all
        plan_ref[0, (side + 1) * room - 1] = found[side]
    for copy in copies:
        copy.wait()


def turn_kernel(plan_ref, right_ref, turned_ref):
    room = plan_ref.shape[1] // 2
    for side in range(2):

        def turn(index, carried, side=side):
            for inner in range(GROUP // 2):
                pair = plan_ref[0, side * room + index * (GROUP // 2) + inner]
                turned_ref[pair] = right_ref[pair].T
            return carried

        lax.fori_loop(0, (plan_ref[0, (side + 1) * room - 1] + GROUP // 2) // (GROUP // 2), turn, 0)


def turned(plan, rights):
    return pl.pallas_call(
        turn_kernel,
        out_shape=kept(rights.shape, rights.dtype),
        in_specs=[SMEM, VMEM],
        out_specs=VMEM,
        compiler_params=params(4),
        cost_estimate=pl.CostEstimate(flops=0, bytes_accessed=8 << 20, transcendentals=0),
    )(plan, pinned(rights))


def make_plan(me, shifts, active, lefts, rights, blocks_dev):
    terms, blocks_all = active.shape
    room = terms * blocks_all + GROUP + 1
    far = pl.BlockSpec(memory_space=pltpu.HBM)
    return pl.pallas_call(
        functools.partial(plan_kernel, blocks_dev),
        out_shape=[
            jax.ShapeDtypeStruct((5, 2 * room), jnp.int32),
            kept(lefts.shape, lefts.dtype),
            kept(rights.shape, rights.dtype),
        ],
        in_specs=[SMEM] * 3 + [far] * 2,
        out_specs=[SMEM, VMEM, VMEM],
        scratch_shapes=[pltpu.SemaphoreType.DMA((2,))],
        compiler_params=params(4),
        cost_estimate=pl.CostEstimate(flops=0, bytes_accessed=16 << 20, transcendentals=0),
    )(me, *(pltpu.with_memory_space_constraint(array, pltpu.HBM) for array in (shifts, active, lefts, rights)))


def pair_product(index, plan_ref, left_ref, right_ref, low_ref):
    pair = plan_ref[0, index]
    half = jnp.dot(left_ref[pair], low_ref[plan_ref[1, index]], preferred_element_type=wide_type).astype(low_type)
    return jnp.dot(half, right_ref[pair], preferred_element_type=wide_type)


def fill_low(first, chunk_refs, own_ref, old_refs, low_ref, fresh_ref, count):
    rows = own_ref.shape[0]
    width = own_ref.shape[1]
    if first:
        for place, chunk_ref in enumerate(chunk_refs):
            blocks = rows // width
            low_ref[place * blocks : (place + 1) * blocks] = chunk_ref[...].reshape(blocks, width, width)
        return
    tails = sum(ref[rows:, :].astype(wide_type) for ref in chunk_refs)

    def total(which):
        return tails[3 * which : 3 * which + 1] + tails[3 * which + 1 : 3 * which + 2] + tails[3 * which + 2 : 3 * which + 3]

    squares, cross, applied_squares = total(0), total(1), total(2)
    rho = cross / squares
    length = squares + step_size * step_size * (applied_squares - rho * cross)
    scale = jnp.sqrt(count / length)
    keep = scale * (1.0 + step_size * rho)
    take = scale * step_size
    for place, chunk_ref in enumerate(chunk_refs):
        source = own_ref if place == 0 else chunk_ref

        def strip(part, carried, place=place, source=source):
            start = pl.multiple_of(part * STRIP, STRIP)
            if len(old_refs) == 1:
                old = old_refs[0][pl.ds(place * rows + start, STRIP), :]
            else:
                old = old_refs[place][pl.ds(start, STRIP), :].astype(wide_type)
            new = keep * old - take * source[pl.ds(start, STRIP), :].astype(wide_type)
            if fresh_ref is not None:
                fresh_ref[pl.ds(place * rows + start, STRIP), :] = new
            low = new.astype(low_type)
            at = place * rows + start
            low_ref[at // width, pl.ds(pl.multiple_of(at % width, STRIP), STRIP), :] = low
            return carried

        lax.fori_loop(0, rows // STRIP, strip, 0, unroll=True)


def grouped(side, plan_ref, left_ref, right_ref, low_ref, take):
    room = plan_ref.shape[1] // 2

    def group(index, carried):
        first = side * room + index * GROUP
        products = [pair_product(first + inner, plan_ref, left_ref, right_ref, low_ref) for inner in range(GROUP)]
        for inner, product in enumerate(products):
            take(first + inner, product)
        return carried

    lax.fori_loop(0, (plan_ref[0, (side + 1) * room - 1] + GROUP - 1) // GROUP, group, 0)


def add_terms(side, term_scale, plan_ref, left_ref, right_ref, low_ref, piece_refs, sum_ref):
    rows, width = piece_refs[0].shape
    blocks = rows // width
    sum_ref[...] = jnp.zeros_like(sum_ref)

    def take(place, product):
        sum_ref[plan_ref[2, place]] += product

    grouped(side, plan_ref, left_ref, right_ref, low_ref, take)
    for place, piece_ref in enumerate(piece_refs):
        piece = sum_ref[place * blocks : (place + 1) * blocks].reshape(rows, width) * term_scale
        piece_ref[...] = piece.astype(piece_ref.dtype)


def far_kernel(first, devices, olds, count, term_scale, *refs):
    plan_ref, left_ref, right_ref = refs[:3]
    chunk_refs = refs[3 : 3 + devices]
    own_ref = refs[3 + devices]
    old_refs = refs[4 + devices : 4 + devices + olds]
    piece_ref, low_ref, *rest, sum_ref = refs[4 + devices + olds :]
    rows, width = own_ref.shape
    fresh_ref = None if first else rest[0]
    fill_low(first, chunk_refs, own_ref, old_refs, low_ref, fresh_ref, count)
    if not first:
        own_low_ref, own_wide_ref = rest[1:]
        own_low_ref[...] = low_ref[: rows // width].reshape(rows, width)
        own_wide_ref[...] = fresh_ref[:rows, :]
    add_terms(0, term_scale, plan_ref, left_ref, right_ref, low_ref, [piece_ref], sum_ref)


def near_kernel(term_scale, plan_ref, left_ref, right_ref, low_ref, *refs):
    *piece_refs, sum_ref = refs
    add_terms(1, term_scale, plan_ref, left_ref, right_ref, low_ref, piece_refs, sum_ref)


def apply_terms(plan, lefts, rights, chunks, own, olds, count, term_scale):
    first = not olds
    devices = len(chunks)
    rows, width = own.shape
    blocks = rows // width
    total = devices * rows
    blocks_all = total // width
    outs = [kept((rows, width), low_type), kept((blocks_all, width, width), low_type)]
    if not first:
        outs += [kept((total, width), wide_type), kept((rows, width), low_type), kept((rows, width), wide_type)]
    cost = pl.CostEstimate(flops=lefts.shape[0] * width**3, bytes_accessed=4 << 20, transcendentals=0)
    sent = pl.pallas_call(
        functools.partial(far_kernel, first, devices, len(olds), count, term_scale),
        out_shape=outs,
        in_specs=[SMEM] + [VMEM] * (3 + devices + len(olds)),
        out_specs=[VMEM] * len(outs),
        scratch_shapes=[pltpu.VMEM((blocks + 1, width, width), wide_type)],
        compiler_params=params(12),
        cost_estimate=cost,
    )(plan, *map(pinned, (lefts, rights, *chunks, own, *olds)))
    last, low, *current = sent
    pieces = pl.pallas_call(
        functools.partial(near_kernel, term_scale),
        out_shape=[kept((rows, width), low_type if place % 2 else wide_type) for place in range(devices - 1)],
        in_specs=[SMEM] + [VMEM] * 3,
        out_specs=[VMEM] * (devices - 1),
        scratch_shapes=[pltpu.VMEM((blocks_all - blocks + 1, width, width), wide_type)],
        compiler_params=params(12),
        cost_estimate=cost,
    )(plan, *map(pinned, (lefts, rights, low)))
    return [*pieces, last], current


def values_kernel(devices, olds, count, *refs):
    plan_ref, left_ref, right_ref = refs[:3]
    chunk_refs = refs[3 : 3 + devices]
    own_ref = refs[3 + devices]
    old_refs = refs[4 + devices : 4 + devices + olds]
    state_ref, value_ref, low_ref, sum_ref = refs[4 + devices + olds :]
    rows, width = own_ref.shape
    blocks = rows // width
    fill_low(False, chunk_refs, own_ref, old_refs, low_ref, None, count)
    state_ref[...] = low_ref[:blocks].reshape(rows, width)
    low_ref[devices * blocks] = jnp.zeros((width, width), low_type)
    sum_ref[...] = jnp.zeros_like(sum_ref)

    def take(place, product):
        target = low_ref[plan_ref[4, place]].astype(wide_type)
        folded = (product * target).reshape(width // 8, 8, width).sum(axis=0)
        sum_ref[plan_ref[3, place]] += folded

    for side in range(2):
        grouped(side, plan_ref, left_ref, right_ref, low_ref, take)
    for term in range(value_ref.shape[1]):
        value_ref[0, term] = jnp.sum(sum_ref[term]) * (1.0 / count)


def term_values(plan, lefts, rights, chunks, own, olds, count, terms):
    devices = len(chunks)
    rows, width = own.shape
    total = devices * rows
    pairs_all = lefts.shape[0]
    return pl.pallas_call(
        functools.partial(values_kernel, devices, len(olds), count),
        out_shape=[jax.ShapeDtypeStruct((rows, width), low_type), jax.ShapeDtypeStruct((1, terms), wide_type)],
        in_specs=[SMEM] + [VMEM] * (3 + devices + len(olds)),
        out_specs=[VMEM, SMEM],
        scratch_shapes=[
            pltpu.VMEM((total // width + 1, width, width), low_type),
            pltpu.VMEM((terms + 1, 8, width), wide_type),
        ],
        compiler_params=params(12),
        cost_estimate=pl.CostEstimate(flops=2 * pairs_all * width**3, bytes_accessed=4 << 20, transcendentals=0),
    )(plan, *map(pinned, (lefts, rights, *chunks, own, *olds)))


def coupling_kernel(own_ref, before_ref, after_ref, out_ref):
    rows, width = own_ref.shape
    for block in range(rows // width):
        at = pl.ds(block * width, width)
        gram = sum(
            lax.dot_general(ref[at, :], ref[at, :], (((0,), (0,)), ((), ())), preferred_element_type=wide_type)
            for ref in (before_ref, after_ref)
        )
        out_ref[at, :] = jnp.dot(
            own_ref[at, :].astype(wide_type), gram, precision=lax.Precision.HIGHEST, preferred_element_type=wide_type
        ) * (0.5 / width)


def coupling(own, before, after):
    rows, width = own.shape
    return pl.pallas_call(
        coupling_kernel,
        out_shape=kept(own.shape, wide_type),
        in_specs=[VMEM] * 3,
        out_specs=VMEM,
        compiler_params=params(4),
        cost_estimate=pl.CostEstimate(flops=0, bytes_accessed=0, transcendentals=0),
    )(*map(pinned, (own, before, after)))


def parts_kernel(*refs):
    *part_refs, out_ref = refs
    for start in range(0, out_ref.shape[0], STRIP):
        at = pl.ds(start, STRIP)
        out_ref[at, :] = sum(ref[at, :].astype(wide_type) for ref in part_refs)


def added(parts):
    shape = parts[0].shape
    return pl.pallas_call(
        parts_kernel,
        out_shape=kept(shape, wide_type),
        in_specs=[VMEM] * len(parts),
        out_specs=VMEM,
        compiler_params=params(4),
        cost_estimate=pl.CostEstimate(flops=1 << 37, bytes_accessed=1 << 24, transcendentals=0),
    )(*map(pinned, parts))


def total_kernel(own_ref, coupled_ref, part_ref, applied_ref, sent_ref):
    rows, width = own_ref.shape
    sums = [jnp.zeros((8, width), wide_type)] * 3
    for start in range(0, rows, STRIP):
        at = pl.ds(start, STRIP)
        applied = coupled_ref[at, :] + part_ref[at, :]
        own = own_ref[at, :].astype(wide_type)
        applied_ref[at, :] = applied
        sent_ref[at, :] = applied.astype(low_type)
        for which, product in enumerate((own * own, own * applied, applied * applied)):
            sums[which] = sums[which] + product.reshape(STRIP // 8, 8, width).sum(axis=0)
    row = lax.broadcasted_iota(jnp.int32, (TAIL, width), 0)
    tail = jnp.zeros((TAIL, width), wide_type)
    for which in range(3):
        rest = jnp.full((TAIL, width), jnp.sum(sums[which]))
        for digit in range(3):
            rounded = rest.astype(low_type).astype(wide_type)
            tail = jnp.where(row == 3 * which + digit, rounded, tail)
            rest = rest - rounded
    sent_ref[rows:, :] = tail.astype(low_type)


def total_applied(own, coupled, part):
    rows, width = own.shape
    return pl.pallas_call(
        total_kernel,
        out_shape=[kept((rows, width), wide_type), kept((rows + TAIL, width), low_type)],
        in_specs=[VMEM] * 3,
        out_specs=[VMEM] * 2,
        compiler_params=params(4),
        cost_estimate=pl.CostEstimate(flops=10 * rows * width, bytes_accessed=rows * width * 16, transcendentals=0),
    )(*map(pinned, (own, coupled, part)))


def shards(psi_start, left_ops, right_ops, shifts, active):
    devices = lax.axis_size("op")
    terms, blocks_all, width = left_ops.shape[1:4]
    blocks_dev = psi_start.shape[1]
    rows = blocks_dev * width
    count = float(blocks_all * width * width)
    term_scale = 1.0 / (terms * devices)
    own_low = psi_start.reshape(rows, width)
    own_wide = own_low
    me = lax.axis_index("op").astype(jnp.int32).reshape(1)
    lefts = left_ops.reshape(terms * blocks_all, width, width)
    rights = right_ops.reshape(terms * blocks_all, width, width)
    plan, lefts, rights = make_plan(me, shifts, active[0], lefts, rights, blocks_dev)
    rights = turned(plan, rights)
    chunks = gathered(own_low, [plan])
    own_source = own_low
    olds = []
    for sweep_index in range(ITERS):
        pieces, current = apply_terms(plan, lefts, rights, chunks, own_source, olds, count, term_scale)
        if olds:
            fresh, own_low, own_wide = current
            olds = [fresh]
        else:
            olds = chunks
        parts, arrived = summed(pieces)
        around = neighbours(after(own_low, [arrived[6]]))
        coupled = coupling(own_wide, *around)
        own_source, sent = total_applied(own_wide, coupled, added(parts))
        chunks = gathered(sent)
    state, values = term_values(plan, lefts, rights, chunks, own_source, olds, count, terms)
    return state.reshape(psi_start.shape), values


def solution(mesh):
    return jax.shard_map(
        shards,
        mesh=mesh,
        in_specs=(
            P("seg", "op", None, None),
            P("seg", "op", None, None, None),
            P("seg", "op", None, None, None),
            P("seg", "op"),
            P("seg", "op", None),
        ),
        out_specs=(P("seg", "op", None, None), P("seg", "op")),
        check_vma=False,
    )
```

```python
import functools

import jax
import jax.numpy as jnp
from jax import lax
from jax.experimental import pallas as pl
from jax.experimental.pallas import tpu as pltpu
from jax.sharding import PartitionSpec as P

ITERS = 3
GROUP = 8
TAIL = 16
STRIP = 64
GATHER_BY = {7: 2}
GATHER_AFTER = {3: (1,), 6: (2,)}
SUM_AFTER = {3: (7,)}

step_size = 0.3
low_type = jnp.bfloat16
wide_type = jnp.float32
VMEM = pl.BlockSpec(memory_space=pltpu.VMEM)
SMEM = pl.BlockSpec(memory_space=pltpu.SMEM)


def params(megabytes):
    return pltpu.CompilerParams(vmem_limit_bytes=megabytes << 20)


def pinned(array):
    return pltpu.with_memory_space_constraint(array, pltpu.VMEM)


def kept(shape, dtype):
    return pltpu.VMEM(shape, dtype)


def traded(block, distance):
    route = [(i, i ^ distance) for i in range(lax.axis_size("op"))]
    return lax.ppermute(block, "op", route)


def neighbours(block):
    devices = lax.axis_size("seg")
    found = []
    for first in (0, 1):
        pairs = [(i, i + 1) for i in range(first, devices - 1, 2)]
        found.append(lax.ppermute(block, "seg", pairs + [(j, i) for i, j in pairs]))
    return found


def hop(place, special={}):
    return special.get(place, place & -place)


def depth(place):
    return place.bit_count()


def after(array, others):
    return lax.optimization_barrier((array, *others))[0] if others else array


def gathered(block, meanwhile=()):
    devices = lax.axis_size("op")
    held = {0: block}
    for place in sorted(range(1, devices), key=depth):
        source = held[place ^ hop(place, GATHER_BY)]
        others = [held[other] for other in GATHER_AFTER.get(place, ())]
        if place in (5, 6):
            others += list(meanwhile)
        source = after(source, others)
        held[place] = traded(source, hop(place, GATHER_BY))
    return [held[place] for place in range(devices)]


def summed(pieces):
    devices = len(pieces)
    came = {place: [] for place in range(devices)}
    arrived = {}
    for place in sorted(range(1, devices), key=lambda place: (depth(place), place), reverse=True):
        piece = pieces[place]
        step = hop(place)
        if came[place]:
            piece = sum((part.astype(wide_type) for part in came[place]), piece.astype(wide_type)).astype(low_type)
        piece = after(piece, [arrived[other] for other in SUM_AFTER.get(place, ())])
        arrived[place] = traded(piece, step)
        came[place ^ step].append(arrived[place])
    return [pieces[0], *came[0][::-1]], arrived


def plan_kernel(blocks_dev, me_ref, shifts_ref, active_ref, left_hbm, right_hbm, plan_ref, left_ref, right_ref, arrived):
    copies = [
        pltpu.make_async_copy(left_hbm, left_ref, arrived.at[0]),
        pltpu.make_async_copy(right_hbm, right_ref, arrived.at[1]),
    ]
    for copy in copies:
        copy.start()
    terms, blocks_all = active_ref.shape
    room = plan_ref.shape[1] // 2
    mine = me_ref[0] * blocks_dev
    bits = blocks_dev.bit_length() - 1
    last = blocks_all // blocks_dev - 1
    found = (0, 0)
    for term in range(terms):
        shift = shifts_ref[0, term]

        def one(block, found, term=term, shift=shift):
            target = block + shift
            target = jnp.where(target >= blocks_all, target - blocks_all, target) ^ mine
            ahead = ((target >> bits) == last).astype(jnp.int32)
            at = jnp.where(ahead == 1, found[0], room + found[1])
            plan_ref[0, at] = term * blocks_all + block
            plan_ref[1, at] = block ^ mine
            plan_ref[2, at] = target - ahead * (last * blocks_dev)
            plan_ref[3, at] = term
            plan_ref[4, at] = target
            is_active = active_ref[term, block]
            counted = is_active & ahead
            return found[0] + counted, found[1] + is_active - counted

        found = lax.fori_loop(0, blocks_all, one, found, unroll=8)
    for side in range(2):
        for extra in range(GROUP):
            at = side * room + found[side] + extra
            plan_ref[0, at] = 0
            plan_ref[1, at] = 0
            plan_ref[2, at] = (1, last)[side] * blocks_dev
            plan_ref[3, at] = terms
            plan_ref[4, at] = blocks_all
        plan_ref[0, (side + 1) * room - 1] = found[side]
    for copy in copies:
        copy.wait()


def turn_kernel(plan_ref, right_ref, turned_ref):
    room = plan_ref.shape[1] // 2
    for side in range(2):

        def turn(index, carried, side=side):
            for inner in range(GROUP // 2):
                pair = plan_ref[0, side * room + index * (GROUP // 2) + inner]
                turned_ref[pair] = right_ref[pair].T
            return carried

        lax.fori_loop(0, (plan_ref[0, (side + 1) * room - 1] + GROUP // 2) // (GROUP // 2), turn, 0)


def turned(plan, rights):
    return pl.pallas_call(
        turn_kernel,
        out_shape=kept(rights.shape, rights.dtype),
        in_specs=[SMEM, VMEM],
        out_specs=VMEM,
        compiler_params=params(4),
        cost_estimate=pl.CostEstimate(flops=0, bytes_accessed=8 << 20, transcendentals=0),
    )(plan, pinned(rights))


def make_plan(me, shifts, active, lefts, rights, blocks_dev):
    terms, blocks_all = active.shape
    room = terms * blocks_all + GROUP + 1
    far = pl.BlockSpec(memory_space=pltpu.HBM)
    return pl.pallas_call(
        functools.partial(plan_kernel, blocks_dev),
        out_shape=[
            jax.ShapeDtypeStruct((5, 2 * room), jnp.int32),
            kept(lefts.shape, lefts.dtype),
            kept(rights.shape, rights.dtype),
        ],
        in_specs=[SMEM] * 3 + [far] * 2,
        out_specs=[SMEM, VMEM, VMEM],
        scratch_shapes=[pltpu.SemaphoreType.DMA((2,))],
        compiler_params=params(4),
        cost_estimate=pl.CostEstimate(flops=0, bytes_accessed=16 << 20, transcendentals=0),
    )(me, *(pltpu.with_memory_space_constraint(array, pltpu.HBM) for array in (shifts, active, lefts, rights)))


def pair_product(index, plan_ref, left_ref, right_ref, low_ref):
    pair = plan_ref[0, index]
    half = jnp.dot(left_ref[pair], low_ref[plan_ref[1, index]], preferred_element_type=wide_type).astype(low_type)
    return jnp.dot(half, right_ref[pair], preferred_element_type=wide_type)


def fill_low(first, chunk_refs, own_ref, old_refs, low_ref, fresh_ref, count):
    rows = own_ref.shape[0]
    width = own_ref.shape[1]
    if first:
        for place, chunk_ref in enumerate(chunk_refs):
            blocks = rows // width
            low_ref[place * blocks : (place + 1) * blocks] = chunk_ref[...].reshape(blocks, width, width)
        return
    tails = sum(ref[rows:, :].astype(wide_type) for ref in chunk_refs)

    def total(which):
        return tails[3 * which : 3 * which + 1] + tails[3 * which + 1 : 3 * which + 2] + tails[3 * which + 2 : 3 * which + 3]

    squares, cross, applied_squares = total(0), total(1), total(2)
    rho = cross / squares
    length = squares + step_size * step_size * (applied_squares - rho * cross)
    scale = jnp.sqrt(count / length)
    keep = scale * (1.0 + step_size * rho)
    take = scale * step_size
    for place, chunk_ref in enumerate(chunk_refs):
        source = own_ref if place == 0 else chunk_ref

        def strip(part, carried, place=place, source=source):
            start = pl.multiple_of(part * STRIP, STRIP)
            if len(old_refs) == 1:
                old = old_refs[0][pl.ds(place * rows + start, STRIP), :]
            else:
                old = old_refs[place][pl.ds(start, STRIP), :].astype(wide_type)
            new = keep * old - take * source[pl.ds(start, STRIP), :].astype(wide_type)
            if fresh_ref is not None:
                fresh_ref[pl.ds(place * rows + start, STRIP), :] = new
            low = new.astype(low_type)
            at = place * rows + start
            low_ref[at // width, pl.ds(pl.multiple_of(at % width, STRIP), STRIP), :] = low
            return carried

        lax.fori_loop(0, rows // STRIP, strip, 0, unroll=True)


def grouped(side, plan_ref, left_ref, right_ref, low_ref, take):
    room = plan_ref.shape[1] // 2
    size = (GROUP // 2, GROUP)[side]

    def group(index, carried):
        first = side * room + index * size
        products = [pair_product(first + inner, plan_ref, left_ref, right_ref, low_ref) for inner in range(size)]
        for inner, product in enumerate(products):
            take(first + inner, product)
        return carried

    lax.fori_loop(0, (plan_ref[0, (side + 1) * room - 1] + size - 1) // size, group, 0)


def add_terms(side, term_scale, plan_ref, left_ref, right_ref, low_ref, piece_refs, sum_ref):
    rows, width = piece_refs[0].shape
    blocks = rows // width
    sum_ref[...] = jnp.zeros_like(sum_ref)

    def take(place, product):
        sum_ref[plan_ref[2, place]] += product

    grouped(side, plan_ref, left_ref, right_ref, low_ref, take)
    for place, piece_ref in enumerate(piece_refs):
        piece = sum_ref[place * blocks : (place + 1) * blocks].reshape(rows, width) * term_scale
        piece_ref[...] = piece.astype(piece_ref.dtype)


def far_kernel(first, devices, olds, count, term_scale, *refs):
    plan_ref, left_ref, right_ref = refs[:3]
    chunk_refs = refs[3 : 3 + devices]
    own_ref = refs[3 + devices]
    old_refs = refs[4 + devices : 4 + devices + olds]
    piece_ref, low_ref, *rest, sum_ref = refs[4 + devices + olds :]
    rows, width = own_ref.shape
    fresh_ref = None if first else rest[0]
    fill_low(first, chunk_refs, own_ref, old_refs, low_ref, fresh_ref, count)
    if not first:
        own_low_ref, own_wide_ref = rest[1:]
        own_low_ref[...] = low_ref[: rows // width].reshape(rows, width)
        own_wide_ref[...] = fresh_ref[:rows, :]
    add_terms(0, term_scale, plan_ref, left_ref, right_ref, low_ref, [piece_ref], sum_ref)


def near_kernel(term_scale, plan_ref, left_ref, right_ref, low_ref, *refs):
    *piece_refs, sum_ref = refs
    add_terms(1, term_scale, plan_ref, left_ref, right_ref, low_ref, piece_refs, sum_ref)


def apply_terms(plan, lefts, rights, chunks, own, olds, count, term_scale):
    first = not olds
    devices = len(chunks)
    rows, width = own.shape
    blocks = rows // width
    total = devices * rows
    blocks_all = total // width
    outs = [kept((rows, width), low_type), kept((blocks_all, width, width), low_type)]
    if not first:
        outs += [kept((total, width), wide_type), kept((rows, width), low_type), kept((rows, width), wide_type)]
    cost = pl.CostEstimate(flops=lefts.shape[0] * width**3, bytes_accessed=4 << 20, transcendentals=0)
    sent = pl.pallas_call(
        functools.partial(far_kernel, first, devices, len(olds), count, term_scale),
        out_shape=outs,
        in_specs=[SMEM] + [VMEM] * (3 + devices + len(olds)),
        out_specs=[VMEM] * len(outs),
        scratch_shapes=[pltpu.VMEM((blocks + 1, width, width), wide_type)],
        compiler_params=params(12),
        cost_estimate=cost,
    )(plan, *map(pinned, (lefts, rights, *chunks, own, *olds)))
    last, low, *current = sent
    pieces = pl.pallas_call(
        functools.partial(near_kernel, term_scale),
        out_shape=[kept((rows, width), low_type if place % 2 else wide_type) for place in range(devices - 1)],
        in_specs=[SMEM] + [VMEM] * 3,
        out_specs=[VMEM] * (devices - 1),
        scratch_shapes=[pltpu.VMEM((blocks_all - blocks + 1, width, width), wide_type)],
        compiler_params=params(12),
        cost_estimate=cost,
    )(plan, *map(pinned, (lefts, rights, low)))
    return [*pieces, last], current


def values_kernel(devices, olds, count, *refs):
    plan_ref, left_ref, right_ref = refs[:3]
    chunk_refs = refs[3 : 3 + devices]
    own_ref = refs[3 + devices]
    old_refs = refs[4 + devices : 4 + devices + olds]
    state_ref, value_ref, low_ref, sum_ref = refs[4 + devices + olds :]
    rows, width = own_ref.shape
    blocks = rows // width
    fill_low(False, chunk_refs, own_ref, old_refs, low_ref, None, count)
    state_ref[...] = low_ref[:blocks].reshape(rows, width)
    low_ref[devices * blocks] = jnp.zeros((width, width), low_type)
    sum_ref[...] = jnp.zeros_like(sum_ref)

    def take(place, product):
        target = low_ref[plan_ref[4, place]].astype(wide_type)
        folded = (product * target).reshape(width // 8, 8, width).sum(axis=0)
        sum_ref[plan_ref[3, place]] += folded

    for side in range(2):
        grouped(side, plan_ref, left_ref, right_ref, low_ref, take)
    for term in range(value_ref.shape[1]):
        value_ref[0, term] = jnp.sum(sum_ref[term]) * (1.0 / count)


def term_values(plan, lefts, rights, chunks, own, olds, count, terms):
    devices = len(chunks)
    rows, width = own.shape
    total = devices * rows
    pairs_all = lefts.shape[0]
    return pl.pallas_call(
        functools.partial(values_kernel, devices, len(olds), count),
        out_shape=[jax.ShapeDtypeStruct((rows, width), low_type), jax.ShapeDtypeStruct((1, terms), wide_type)],
        in_specs=[SMEM] + [VMEM] * (3 + devices + len(olds)),
        out_specs=[VMEM, SMEM],
        scratch_shapes=[
            pltpu.VMEM((total // width + 1, width, width), low_type),
            pltpu.VMEM((terms + 1, 8, width), wide_type),
        ],
        compiler_params=params(12),
        cost_estimate=pl.CostEstimate(flops=2 * pairs_all * width**3, bytes_accessed=4 << 20, transcendentals=0),
    )(plan, *map(pinned, (lefts, rights, *chunks, own, *olds)))


def coupling_kernel(own_ref, before_ref, after_ref, out_ref):
    rows, width = own_ref.shape
    for block in range(rows // width):
        at = pl.ds(block * width, width)
        gram = sum(
            lax.dot_general(ref[at, :], ref[at, :], (((0,), (0,)), ((), ())), preferred_element_type=wide_type)
            for ref in (before_ref, after_ref)
        )
        out_ref[at, :] = jnp.dot(
            own_ref[at, :].astype(wide_type), gram, precision=lax.Precision.HIGHEST, preferred_element_type=wide_type
        ) * (0.5 / width)


def coupling(own, before, after):
    rows, width = own.shape
    return pl.pallas_call(
        coupling_kernel,
        out_shape=kept(own.shape, wide_type),
        in_specs=[VMEM] * 3,
        out_specs=VMEM,
        compiler_params=params(4),
        cost_estimate=pl.CostEstimate(flops=0, bytes_accessed=0, transcendentals=0),
    )(*map(pinned, (own, before, after)))


def parts_kernel(*refs):
    *part_refs, out_ref = refs
    for start in range(0, out_ref.shape[0], STRIP):
        at = pl.ds(start, STRIP)
        out_ref[at, :] = sum(ref[at, :].astype(wide_type) for ref in part_refs)


def added(parts):
    shape = parts[0].shape
    return pl.pallas_call(
        parts_kernel,
        out_shape=kept(shape, wide_type),
        in_specs=[VMEM] * len(parts),
        out_specs=VMEM,
        compiler_params=params(4),
        cost_estimate=pl.CostEstimate(flops=1 << 37, bytes_accessed=1 << 24, transcendentals=0),
    )(*map(pinned, parts))


def total_kernel(own_ref, coupled_ref, part_ref, applied_ref, sent_ref):
    rows, width = own_ref.shape
    sums = [jnp.zeros((8, width), wide_type)] * 3
    for start in range(0, rows, STRIP):
        at = pl.ds(start, STRIP)
        applied = coupled_ref[at, :] + part_ref[at, :]
        own = own_ref[at, :].astype(wide_type)
        applied_ref[at, :] = applied
        sent_ref[at, :] = applied.astype(low_type)
        for which, product in enumerate((own * own, own * applied, applied * applied)):
            sums[which] = sums[which] + product.reshape(STRIP // 8, 8, width).sum(axis=0)
    row = lax.broadcasted_iota(jnp.int32, (TAIL, width), 0)
    tail = jnp.zeros((TAIL, width), wide_type)
    for which in range(3):
        rest = jnp.full((TAIL, width), jnp.sum(sums[which]))
        for digit in range(3):
            rounded = rest.astype(low_type).astype(wide_type)
            tail = jnp.where(row == 3 * which + digit, rounded, tail)
            rest = rest - rounded
    sent_ref[rows:, :] = tail.astype(low_type)


def total_applied(own, coupled, part):
    rows, width = own.shape
    return pl.pallas_call(
        total_kernel,
        out_shape=[kept((rows, width), wide_type), kept((rows + TAIL, width), low_type)],
        in_specs=[VMEM] * 3,
        out_specs=[VMEM] * 2,
        compiler_params=params(4),
        cost_estimate=pl.CostEstimate(flops=10 * rows * width, bytes_accessed=rows * width * 16, transcendentals=0),
    )(*map(pinned, (own, coupled, part)))


def shards(psi_start, left_ops, right_ops, shifts, active):
    devices = lax.axis_size("op")
    terms, blocks_all, width = left_ops.shape[1:4]
    blocks_dev = psi_start.shape[1]
    rows = blocks_dev * width
    count = float(blocks_all * width * width)
    term_scale = 1.0 / (terms * devices)
    own_low = psi_start.reshape(rows, width)
    own_wide = own_low
    me = lax.axis_index("op").astype(jnp.int32).reshape(1)
    lefts = left_ops.reshape(terms * blocks_all, width, width)
    rights = right_ops.reshape(terms * blocks_all, width, width)
    plan, lefts, rights = make_plan(me, shifts, active[0], lefts, rights, blocks_dev)
    rights = turned(plan, rights)
    chunks = gathered(own_low, [plan])
    own_source = own_low
    olds = []
    for sweep_index in range(ITERS):
        pieces, current = apply_terms(plan, lefts, rights, chunks, own_source, olds, count, term_scale)
        if olds:
            fresh, own_low, own_wide = current
            olds = [fresh]
        else:
            olds = chunks
        parts, arrived = summed(pieces)
        around = neighbours(after(own_low, [arrived[6]]))
        coupled = coupling(own_wide, *around)
        own_source, sent = total_applied(own_wide, coupled, added(parts))
        chunks = gathered(sent)
    state, values = term_values(plan, lefts, rights, chunks, own_source, olds, count, terms)
    return state.reshape(psi_start.shape), values


def solution(mesh):
    return jax.shard_map(
        shards,
        mesh=mesh,
        in_specs=(
            P("seg", "op", None, None),
            P("seg", "op", None, None, None),
            P("seg", "op", None, None, None),
            P("seg", "op"),
            P("seg", "op", None),
        ),
        out_specs=(P("seg", "op", None, None), P("seg", "op")),
        check_vma=False,
    )
```
